256 devices in a mesh: blk: 32 (over z, y), feat: 8 (over x, core).
Axes of the slice: x: 4, y: 4, z: 8, core: 2. Of those that a mesh axis runs over, the one named last changes fastest.
Arguments:
- features: bfloat16 [262144, 256], P('blk', 'feat'), may hold values from -6 to 6
- tile_cols: int32 [2048, 16], P('blk'), may hold values from 0 to 2047, as said below
- tile_count: int32 [2048], P('blk'), may hold values from 1 to 16, as said below
- edge_mask: int32 [2048, 16, 128, 128], P('blk'), may hold values 0 or 1
- weight: bfloat16 [256, 256], replicated, may hold values from -0.375 to 0.375
- bias: float32 [256], replicated, may hold values from -3 to 3
Outputs:
- result: bfloat16 [262144, 256], P(('blk', 'feat'))
The draws below stay inside these ranges and needn't reach their ends.
Inputs may be any that keep to these rules, and one draw needn't show every extreme that they name: `tile_cols`: the slots of a row name distinct column blocks. A block c lies with owner c // 64; every column block of row b has an owner within 2 of b // 64, counted cyclically over the blk axis, and among the slots in use of every row one is exactly 2 away. `tile_count`: some block row uses all 16 slots.
All inputs are finite; a program needn't handle non-finite values. Where the reference program divides by a largest or mean magnitude, that divisor is 1e-20 or more. No bound on the sum of `edge_mask` on one device may be relied on, other than what follows from the above.
Results may differ from the reference program's by a relative error of at most 0.0075.
Values may be sent and summed in bfloat16 or wider, within the bound.
A program may use at most 192 MiB of HBM per device.

```python
import jax
import jax.numpy as jnp
from jax import lax

F = 256
FO = 256
TILE = 128
TMAX = 16
REACH = 2
NBR = 64
NBLK = 2048
N = 262144


def tile_layout(key):
    count_key = jax.random.fold_in(key, 11)
    full_key = jax.random.fold_in(key, 12)
    row_key = jax.random.fold_in(key, 13)
    counts = jax.random.randint(count_key, (NBLK,), 1, TMAX + 1)
    where_full = jax.random.randint(full_key, (), 0, NBLK)
    counts = counts.at[where_full].set(TMAX).astype(jnp.int32)
    window = (2 * REACH + 1) * NBR

    def one_row(row_index, row_count):
        base = jax.random.fold_in(row_key, row_index)
        scores = jax.random.permutation(jax.random.fold_in(base, 1), window).astype(jnp.int32)
        side = jax.random.randint(jax.random.fold_in(base, 2), (), 0, 2)
        offset = jax.random.randint(jax.random.fold_in(base, 3), (), 0, NBR)
        far_slot = side * (2 * REACH * NBR) + offset
        scores = scores.at[far_slot].set(-1)
        order = jnp.argsort(scores, stable=True).astype(jnp.int32)[:TMAX]
        spot = jax.random.randint(jax.random.fold_in(base, 4), (), 0, row_count)
        order = jnp.roll(order, spot)
        owner = row_index // NBR
        return ((owner - REACH) * NBR + order) % NBLK
    rows = jnp.arange(NBLK, dtype=jnp.int32)
    columns = jax.vmap(one_row)(rows, counts)
    return (columns.astype(jnp.int32), counts)


def draw_tile_cols(key, part):
    columns, counts = tile_layout(key)
    return columns


def draw_tile_count(key, part):
    columns, counts = tile_layout(key)
    return counts


def plant(values, own_key, smallest, high):
    shape = values.shape
    place = [jax.random.randint(jax.random.fold_in(own_key, axis), (), 0, shape[axis]) for axis in range(len(shape))]
    values = values.at[tuple(place)].set(smallest)
    longest = shape.index(max(shape))
    place[longest] = (place[longest] + 1) % shape[longest]
    return values.at[tuple(place)].set(high)


def block_levels(own_key, shape, cuts, low, top_value):
    factor_of, own = 1.0, jax.random.fold_in(own_key, 6)
    for position, blocks in cuts:
        draws = jnp.exp(jax.random.uniform(jax.random.fold_in(own, position), (blocks,), jnp.float32, low / len(cuts), top_value / len(cuts)))
        factor_of = factor_of * jnp.repeat(draws, shape[position] // blocks).reshape([-1 if axis == position else 1 for axis in range(len(shape))])
    return factor_of


def bell_draw(own_key, extent, deviation, limit, shards=(), kind=jnp.bfloat16):
    array = deviation * jax.random.normal(own_key, extent, jnp.float32)
    if shards:
        array = array * block_levels(own_key, extent, shards, -0.22, 0.18)
    return jnp.clip(array, -limit, limit).astype(kind)


def setup_inputs(seed: int = 0) -> dict:
    seeds = jax.random.split(jax.random.key(seed), 7)
    features = bell_draw(seeds[0], (N, F), 1.0, 6.0, ((0, 32), (1, 8)))
    tile_cols = draw_tile_cols(jax.random.fold_in(seeds[6], 71), 0)
    tile_count = draw_tile_count(jax.random.fold_in(seeds[6], 71), 0)
    edge_mask = plant((jax.random.randint(seeds[3], (NBLK, TMAX, TILE, TILE), 0, max(2, TILE * (TMAX + 1) // 40)) < 1).astype(jnp.int32), jax.random.fold_in(seeds[3], 1), 0, 1)
    weight = bell_draw(seeds[4], (F, FO), F ** -0.5, 0.375)
    bias = bell_draw(seeds[5], (FO,), 0.5, 3.0, (), jnp.float32)
    return {"features": features, "tile_cols": tile_cols, "tile_count": tile_count, "edge_mask": edge_mask, "weight": weight, "bias": bias}


epsilon = 1e-06

def reference(features, tile_cols, tile_count, edge_mask, weight, bias):
    slot_ids = jnp.arange(TMAX, dtype=jnp.int32)
    active_int = (slot_ids[None, :] < tile_count[:, None]).astype(jnp.int32)
    row_ones = lax.optimization_barrier(jnp.sum(edge_mask, axis=3))
    degree = lax.optimization_barrier(jnp.sum(row_ones * active_int[:, :, None], axis=1)).reshape(N) + 1
    inv_root = lax.rsqrt(degree.astype(jnp.float32))
    scaled = (features.astype(jnp.float32) * inv_root[:, None]).astype(jnp.bfloat16)
    blocks = scaled.reshape(NBLK, TILE, F)

    def one_row(packed):
        columns, tile_num, edges, own_rows = packed
        active = (slot_ids < tile_num).astype(jnp.float32)
        picked = blocks[columns.astype(jnp.int32)].astype(jnp.float32)
        weighted = edges.astype(jnp.float32) * active[:, None, None]
        return jnp.einsum('tij,tjf->if', weighted, picked) + own_rows.astype(jnp.float32)
    summed = lax.map(one_row, (tile_cols, tile_count, edge_mask, blocks))
    aggregate = (summed.reshape(N, F) * inv_root[:, None]).astype(jnp.bfloat16)
    peak_abs = lax.optimization_barrier(jnp.max(jnp.abs(aggregate.astype(jnp.float32)).reshape(NBLK, TILE * F), axis=1))
    normalized = (aggregate.astype(jnp.float32).reshape(NBLK, TILE, F) / (peak_abs + epsilon)[:, None, None]).astype(jnp.bfloat16).reshape(N, F)
    mixed = jnp.dot(normalized, weight, preferred_element_type=jnp.float32) + bias.astype(jnp.float32)
    return jax.nn.relu(mixed).astype(jnp.bfloat16)
```

```python
import functools

import jax
import jax.numpy as jnp
from jax import lax
from jax.experimental import pallas as pl
from jax.experimental.pallas import tpu as pltpu
from jax.sharding import PartitionSpec as P

MESH = pl.DeviceIdType.MESH

TILE = 128
REACH = 2
SPAN = 2 * REACH + 1
epsilon = 1e-06

CORES = 2
ROWS = 64
SLOTS = 16
PART = 32
WIDE = CORES * PART
HALF = ROWS // CORES
GROUP = 8
CHIPS = 4
STAGES = 16
NODES = ROWS * TILE

NT = (((1,), (1,)), ((), ()))
TN = (((0,), (0,)), ((), ()))


def kernel(
    ft, mask, idx, count, weight, bias, out,
    stage, tiles, raw, scaled, inv, degq, degall, aggsend, aggrecv,
    stage_sem, own_sem, panel_send, panel_recv, pair_send, pair_recv,
    degq_send, degq_recv, degall_send, degall_recv, agg_send, agg_recv,
):
    blk = lax.axis_index("blk")
    feat = lax.axis_index("feat")
    owners = lax.axis_size("blk")
    feats = lax.axis_size("feat")
    chip, core = feat // CORES, feat % CORES
    partner = (blk, chip * CORES + 1 - core)

    def owner(d):
        return lax.rem(blk + d + owners, owners)

    def block_row(q):
        j, k = q // GROUP, q % GROUP
        return lax.rem(chip + j, CHIPS) * (CORES * GROUP) + core * GROUP + k

    def stage_copy(q):
        slot = q % STAGES
        return pltpu.make_async_copy(mask.at[block_row(q)], stage.at[slot], stage_sem.at[slot])

    for q in range(STAGES):
        stage_copy(q).start()
    own_copy = pltpu.make_async_copy(ft, raw.at[core, REACH], own_sem)
    own_copy.start()
    scaled[SPAN * ROWS] = jnp.zeros((WIDE, TILE), jnp.bfloat16)

    barrier = pltpu.get_barrier_semaphore()
    offsets = [d for d in range(-REACH, REACH + 1) if d != 0]
    for d in offsets:
        pl.semaphore_signal(barrier, inc=1, device_id=(owner(d), feat), device_id_type=MESH)
    for s in range(1, feats):
        pl.semaphore_signal(barrier, inc=1, device_id=(blk, lax.rem(feat + s, feats)), device_id_type=MESH)
    pl.semaphore_wait(barrier, len(offsets) + feats - 1)

    def panel_copy(d):
        return pltpu.make_async_remote_copy(
            src_ref=ft, dst_ref=raw.at[core, REACH - d],
            send_sem=panel_send.at[REACH - d], recv_sem=panel_recv.at[REACH - d],
            device_id=(owner(d), feat), device_id_type=MESH)

    def pair_copy(slot):
        return pltpu.make_async_remote_copy(
            src_ref=ft if slot == REACH else raw.at[core, slot], dst_ref=raw.at[core, slot],
            send_sem=pair_send.at[slot], recv_sem=pair_recv.at[slot],
            device_id=partner, device_id_type=MESH)

    for d in (-2, 2, -1, 1):
        panel_copy(d).start()
    pair_copy(REACH).start()

    def convert(q):
        slot = q % STAGES
        stage_copy(q).wait()
        for t in range(SLOTS):
            tiles[q, :, t * TILE:(t + 1) * TILE] = stage[slot, t].astype(jnp.float32).astype(jnp.bfloat16)

    def own_row(q, _):
        convert(q)
        b = block_row(q)
        n = count[b]
        total = jnp.zeros((TILE, TILE), jnp.int32)
        for t in range(SLOTS):
            total = total + stage[q, t] * (t < n).astype(jnp.int32)
        total = total.astype(jnp.float32).astype(jnp.bfloat16)
        ones = jnp.ones((8, TILE), jnp.bfloat16)
        degree = 1.0 + lax.dot_general(ones, total, NT, preferred_element_type=jnp.float32)
        degq[REACH, pl.ds(q, 1)] = degree[0:1]
        stage_copy(q + STAGES).start()
        return 0

    lax.fori_loop(0, GROUP, own_row, 0)

    def degq_copy(d):
        return pltpu.make_async_remote_copy(
            src_ref=degq.at[REACH], dst_ref=degq.at[REACH - d],
            send_sem=degq_send.at[REACH - d], recv_sem=degq_recv.at[REACH - d],
            device_id=(owner(d), feat), device_id_type=MESH)

    def degall_copy(s):
        return pltpu.make_async_remote_copy(
            src_ref=degq, dst_ref=degall.at[feat],
            send_sem=degall_send.at[s], recv_sem=degall_recv.at[s],
            device_id=(blk, lax.rem(feat + s, feats)), device_id_type=MESH)

    for d in offsets:
        degq_copy(d).start()

    def more_rows(q, _):
        convert(q)

        @pl.when(q < HALF - STAGES)
        def _():
            stage_copy(q + STAGES).start()
        return 0

    lax.fori_loop(GROUP, STAGES, more_rows, 0)

    for d in offsets:
        degq_copy(d).wait()
    for s in range(1, feats):
        degall_copy(s).start()
    degall[feat] = degq[...]

    lax.fori_loop(STAGES, HALF, more_rows, 0)

    for s in range(1, feats):
        degall_copy(s).wait()
    for f in range(feats):
        for d in range(SPAN):
            inv[pl.ds(d * ROWS + f * GROUP, GROUP)] = lax.rsqrt(degall[f, d])

    own_copy.wait()
    pair_copy(REACH).wait()

    def scale(slot):
        def body(c, _):
            at = pl.multiple_of(c * TILE, TILE)
            row = slot * ROWS + c
            factor = inv[pl.ds(row, 1)]
            for h in range(CORES):
                block = raw[h, slot, :, pl.ds(at, TILE)].astype(jnp.float32)
                scaled[row, h * PART:(h + 1) * PART] = (block * factor).astype(jnp.bfloat16)
            return 0
        lax.fori_loop(0, ROWS, body, 0, unroll=4)

    scale(REACH)
    for d in (-1, 1, -2, 2):
        slot = REACH + d
        panel_copy(-d).wait()
        pair_copy(slot).start()
    for d in (-1, 1, -2, 2):
        slot = REACH + d
        pair_copy(slot).wait()
        scale(slot)

    def agg_copy(j):
        return pltpu.make_async_remote_copy(
            src_ref=aggsend.at[j], dst_ref=aggrecv.at[:, pl.ds(pl.multiple_of(chip * WIDE, WIDE), WIDE)],
            send_sem=agg_send.at[j], recv_sem=agg_recv.at[j],
            device_id=(blk, lax.rem(chip + j, CHIPS) * CORES + core), device_id_type=MESH)

    def aggregate(q):
        b = block_row(q)
        total = jnp.zeros((WIDE, TILE), jnp.float32)
        for pair in range(SLOTS // 2):
            left = jnp.concatenate(
                [scaled[idx[b, 2 * pair]], scaled[idx[b, 2 * pair + 1]]], axis=1)
            right = tiles[q, :, pair * 2 * TILE:(pair + 1) * 2 * TILE]
            total = total + lax.dot_general(left, right, NT, preferred_element_type=jnp.float32)
        total = total + scaled[REACH * ROWS + b].astype(jnp.float32)
        return (total * inv[pl.ds(REACH * ROWS + b, 1)]).astype(jnp.bfloat16)

    for j in (2, 1, 3):
        def send_row(k, _, j=j):
            aggsend[j, k] = aggregate(j * GROUP + k)
            return 0
        lax.fori_loop(0, GROUP, send_row, 0)
        agg_copy(j).start()

    def keep_row(k, _):
        aggrecv[k, pl.ds(pl.multiple_of(chip * WIDE, WIDE), WIDE)] = aggregate(k)
        return 0
    lax.fori_loop(0, GROUP, keep_row, 0)

    for j in (2, 1, 3):
        agg_copy(j).wait()

    def finish(k, _):
        values = aggrecv[k].astype(jnp.float32)
        peak_abs = jnp.max(jnp.abs(values))
        normalized = (values / (peak_abs + epsilon)).astype(jnp.bfloat16)
        mixed = lax.dot_general(normalized, weight[...], TN, preferred_element_type=jnp.float32)
        mixed = jnp.maximum(mixed + bias[...], 0.0).astype(jnp.bfloat16)
        out[pl.ds(pl.multiple_of(k * TILE, TILE), TILE)] = mixed
        return 0
    lax.fori_loop(0, GROUP, finish, 0)


def per_device(features, tile_cols, tile_count, edge_mask, weight, bias):
    slot_ids = jnp.arange(SLOTS, dtype=jnp.int32)
    active = slot_ids[None, :] < tile_count[:, None]
    owners = lax.axis_size("blk")
    distance = (tile_cols // ROWS - lax.axis_index("blk") + REACH) % owners
    idx = jnp.where(active, distance * ROWS + tile_cols % ROWS, SPAN * ROWS)
    feats = lax.axis_size("feat")
    smem = pl.BlockSpec(memory_space=pltpu.SMEM)
    vmem = pl.BlockSpec(memory_space=pltpu.VMEM)
    hbm = pl.BlockSpec(memory_space=pl.ANY)
    dma = pltpu.SemaphoreType.DMA
    return pl.pallas_call(
        kernel,
        out_shape=jax.ShapeDtypeStruct((GROUP * TILE, weight.shape[1]), jnp.bfloat16),
        in_specs=[hbm, hbm, smem, smem, vmem, vmem],
        out_specs=vmem,
        scratch_shapes=[
            pltpu.VMEM((STAGES, SLOTS, TILE, TILE), jnp.int32),
            pltpu.VMEM((HALF, TILE, SLOTS * TILE), jnp.bfloat16),
            pltpu.VMEM((CORES, SPAN, PART, NODES), jnp.bfloat16),
            pltpu.VMEM((SPAN * ROWS + 1, WIDE, TILE), jnp.bfloat16),
            pltpu.VMEM((SPAN * ROWS, TILE), jnp.float32),
            pltpu.VMEM((SPAN, GROUP, TILE), jnp.float32),
            pltpu.VMEM((feats, SPAN, GROUP, TILE), jnp.float32),
            pltpu.VMEM((CHIPS, GROUP, WIDE, TILE), jnp.bfloat16),
            pltpu.VMEM((GROUP, CHIPS * WIDE, TILE), jnp.bfloat16),
            dma((STAGES,)), dma, dma((SPAN,)), dma((SPAN,)), dma((SPAN,)), dma((SPAN,)),
            dma((SPAN,)), dma((SPAN,)), dma((feats,)), dma((feats,)), dma((CHIPS,)), dma((CHIPS,)),
        ],
        compiler_params=pltpu.CompilerParams(
            collective_id=0, has_side_effects=True, vmem_limit_bytes=60 * 1024 * 1024),
    )(features.T, edge_mask, idx, tile_count, weight, bias.reshape(1, -1))


def solution(mesh):
    placed = (P("blk", "feat"), P("blk", None), P("blk"), P("blk", None, None, None), P(), P())
    return jax.shard_map(
        per_device, mesh=mesh, in_specs=placed, out_specs=P(("blk", "feat"), None), check_vma=False
    )
```

```python
import functools

import jax
import jax.numpy as jnp
from jax import lax
from jax.experimental import pallas as pl
from jax.experimental.pallas import tpu as pltpu
from jax.sharding import PartitionSpec as P

MESH = pl.DeviceIdType.MESH

TILE = 128
REACH = 2
SPAN = 2 * REACH + 1
epsilon = 1e-06

CORES = 2
ROWS = 64
SLOTS = 16
PART = 32
HALVES = 2
SUB = PART // HALVES
WIDE = CORES * SUB
HALF = ROWS // CORES
GROUP = 8
CHIPS = 4
RING = 4
STAGES = 16
NODES = ROWS * TILE

CHUNKS = 4
TOTAL = HALVES * CHUNKS
BLOCKS = ROWS // CHUNKS
LANES = BLOCKS * TILE
CROSS = (3,)
AHEAD = 2
PASS = SPAN
STEPS = TOTAL + 4
PAIRS = 2
SUBS = GROUP // PAIRS

NT = (((1,), (1,)), ((), ()))
TN = (((0,), (0,)), ((), ()))


def crosses(n):
    return n % CHUNKS in CROSS


def kernel(
    ft, mask, cols, count, weight, bias, out,
    stage, tiles, raw, scaled, inv, degq, degall, aggsend, aggrecv, order,
    stage_sem, own_sem, panel_send, panel_recv, pair_send, pair_recv,
    degq_send, degq_recv, degall_send, degall_recv, agg_send, agg_recv,
):
    blk = lax.axis_index("blk")
    feat = lax.axis_index("feat")
    owners = lax.axis_size("blk")
    feats = lax.axis_size("feat")
    layers = owners // RING
    chip, core = feat // CORES, feat % CORES
    z, y = blk // RING, blk % RING

    mirrored = y >= RING // 2
    place = jnp.where(mirrored, RING - 1 - y, y)
    outer = place == 0
    inner = place == 1
    ahead_z = jnp.where(mirrored, layers - 1, 1)

    def at(zz, yy):
        return (zz * RING + yy, feat)

    near = at(z, jnp.where(mirrored, 2 + place, 1 - place))
    across = at(z, RING - 1 - y)
    up = at(lax.rem(z + ahead_z, layers), y)
    down = at(lax.rem(z + layers - ahead_z, layers), y)
    partner = (blk, chip * CORES + 1 - core)

    def owner(d):
        return lax.rem(blk + d + owners, owners)

    def block_row(q):
        j, k = q // GROUP, q % GROUP
        return lax.rem(chip + j, CHIPS) * (CORES * GROUP) + core * GROUP + k

    def stage_copy(q):
        slot = q % STAGES
        return pltpu.make_async_copy(mask.at[block_row(q)], stage.at[slot], stage_sem.at[slot])

    for q in range(STAGES):
        stage_copy(q).start()
    own_copy = pltpu.make_async_copy(ft, raw.at[core, REACH], own_sem)
    own_copy.start()

    barrier = pltpu.get_barrier_semaphore()
    offsets = [d for d in range(-REACH, REACH + 1) if d != 0]
    peers = [near, across, up, down]
    peers += [(owner(d), feat) for d in offsets]
    peers += [(blk, lax.rem(feat + s, feats)) for s in range(1, feats)]
    for peer in peers:
        pl.semaphore_signal(barrier, inc=1, device_id=peer, device_id_type=MESH)
    pl.semaphore_wait(barrier, len(peers))

    def piece(n):
        h, c = n // CHUNKS, n % CHUNKS
        return pl.ds(h * SUB, SUB), pl.ds(c * LANES, LANES)

    def panel_copy(source, target, n, device, kind):
        features, nodes = piece(n)
        src = ft.at[features, nodes] if source == REACH else raw.at[core, source, features, nodes]
        return pltpu.make_async_remote_copy(
            src_ref=src, dst_ref=raw.at[core, target, features, nodes],
            send_sem=panel_send.at[kind, n], recv_sem=panel_recv.at[target, n],
            device_id=device, device_id_type=MESH)

    def pair_copy(slot, n):
        features, nodes = piece(n)
        here = raw.at[core, slot, features, nodes]
        return pltpu.make_async_remote_copy(
            src_ref=ft.at[features, nodes] if slot == REACH else here, dst_ref=here,
            send_sem=pair_send.at[slot, n], recv_sem=pair_recv.at[slot, n],
            device_id=partner, device_id_type=MESH)

    def arrive(slot, n):
        panel_copy(slot, slot, n, near, 0).wait_recv()

    every, far, close = (lambda n: True), crosses, (lambda n: not crosses(n))
    outer_sends = {
        (REACH, 0): (1, near, every), (REACH, 1): (PASS, across, far), (3, 2): (4, across, every),
        (PASS, 3): (4, near, far), (PASS, 4): (1, up, far), (4, 5): (0, up, every)}
    inner_sends = {
        (REACH, 0): (3, near, every), (REACH, 1): (3, across, every), (1, 2): (4, across, close),
        (4, 3): (0, up, every), (0, 4): (1, near, close)}

    def forward(table, source, n, wait=False):
        for (start, kind), (target, device, which) in table.items():
            if start == source and which(n):
                copy = panel_copy(start, target, n, device, kind)
                if wait:
                    copy.wait_send()
                else:
                    copy.start()

    def send_own(n):
        @pl.when(outer)
        def _():
            forward(outer_sends, REACH, n)

        @pl.when(inner)
        def _():
            forward(inner_sends, REACH, n)
        pair_copy(REACH, n).start()

    def relay(table, slot, n):
        arrive(slot, n)
        forward(table, slot, n)
        if slot != PASS:
            pair_copy(slot, n).start()

    def transfer(step):
        a, b, c, d = step, step - 1, step - 2, step - 3

        @pl.when(outer)
        def _():
            if 0 <= d < TOTAL and not crosses(d):
                relay(outer_sends, 1, d)
            if 0 <= c < TOTAL:
                relay(outer_sends, 0, c)
            if 0 <= b < TOTAL:
                relay(outer_sends, 4, b)
                if crosses(b):
                    relay(outer_sends, 1, b)
            if a < TOTAL:
                if crosses(a):
                    relay(outer_sends, PASS, a)
                relay(outer_sends, 3, a)

        @pl.when(inner)
        def _():
            if 0 <= c < TOTAL:
                relay(inner_sends, 0, c)
            if 0 <= b < TOTAL:
                relay(inner_sends, 4, b)
            if a < TOTAL:
                relay(inner_sends, 1, a)
                relay(inner_sends, 3, a)
        if a + AHEAD < TOTAL:
            send_own(a + AHEAD)

    for n in range(AHEAD):
        send_own(n)

    for h in range(HALVES):
        scaled[h, SPAN * ROWS] = jnp.zeros((WIDE, TILE), jnp.bfloat16)
    for x in range(CHIPS):
        for c in range(CORES):
            for h in range(HALVES):
                source = (x * CORES + c) * PART + h * SUB
                target = (h * CHIPS + x) * WIDE + c * SUB
                order[target:target + SUB] = weight[source:source + SUB]

    def convert(q):
        slot = q % STAGES
        stage_copy(q).wait()
        for t in range(SLOTS):
            tiles[q, :, t * TILE:(t + 1) * TILE] = stage[slot, t].astype(jnp.float32).astype(jnp.bfloat16)

    def own_row(q, _):
        convert(q)
        n = count[block_row(q)]
        total = jnp.zeros((TILE, TILE), jnp.int32)
        for t in range(SLOTS):
            total = total + stage[q, t] * (t < n).astype(jnp.int32)
        total = total.astype(jnp.float32).astype(jnp.bfloat16)
        ones = jnp.ones((8, TILE), jnp.bfloat16)
        degree = 1.0 + lax.dot_general(ones, total, NT, preferred_element_type=jnp.float32)
        degq[REACH, pl.ds(q, 1)] = degree[0:1]
        stage_copy(q + STAGES).start()
        return 0

    def more_row(q, _):
        convert(q)

        @pl.when(q < HALF - STAGES)
        def _():
            stage_copy(q + STAGES).start()
        return 0

    def degq_copy(d):
        return pltpu.make_async_remote_copy(
            src_ref=degq.at[REACH], dst_ref=degq.at[REACH - d],
            send_sem=degq_send.at[REACH - d], recv_sem=degq_recv.at[REACH - d],
            device_id=(owner(d), feat), device_id_type=MESH)

    def degall_copy(s):
        return pltpu.make_async_remote_copy(
            src_ref=degq, dst_ref=degall.at[feat],
            send_sem=degall_send.at[s], recv_sem=degall_recv.at[s],
            device_id=(blk, lax.rem(feat + s, feats)), device_id_type=MESH)

    def scale(n):
        h, c = n // CHUNKS, n % CHUNKS
        for slot in range(SPAN):
            pair_copy(slot, n).wait()
        for slot in range(SPAN):
            there = jnp.where(mirrored, SPAN - 1 - slot, slot) * ROWS

            def body(i, _, slot=slot, there=there):
                block = c * BLOCKS + i
                nodes = pl.ds(pl.multiple_of(block * TILE, TILE), TILE)
                factor = inv[pl.ds(there + block, 1)]
                for k in range(CORES):
                    values = raw[k, slot, h * SUB:(h + 1) * SUB, nodes].astype(jnp.float32)
                    scaled[h, there + block, k * SUB:(k + 1) * SUB] = (values * factor).astype(jnp.bfloat16)
                return 0
            lax.fori_loop(0, BLOCKS, body, 0, unroll=4)

    def agg_copy(h, j, s):
        rows = pl.ds(s * PAIRS, PAIRS)
        return pltpu.make_async_remote_copy(
            src_ref=aggsend.at[h, j, rows], dst_ref=aggrecv.at[rows, h, chip],
            send_sem=agg_send.at[h, j, s], recv_sem=agg_recv.at[h, j, s],
            device_id=(blk, lax.rem(chip + j, CHIPS) * CORES + core), device_id_type=MESH)

    first = (blk - REACH) * ROWS
    blocks = owners * ROWS

    def aggregate(h, q):
        b = block_row(q)
        used = count[b]

        def panel(t):
            local = (cols[t, b] - first + blocks) & (blocks - 1)
            return scaled[h, jnp.where(t < used, local, SPAN * ROWS)]
        total = jnp.zeros((WIDE, TILE), jnp.float32)
        for t in range(0, SLOTS, 2):
            left = jnp.concatenate([panel(t), panel(t + 1)], axis=1)
            right = tiles[q, :, t * TILE:(t + 2) * TILE]
            total = total + lax.dot_general(left, right, NT, preferred_element_type=jnp.float32)
        total = total + scaled[h, REACH * ROWS + b].astype(jnp.float32)
        return (total * inv[pl.ds(REACH * ROWS + b, 1)]).astype(jnp.bfloat16)

    def aggregate_rows(h, s):
        for j in (2, 1, 3):
            def row(k, _, j=j):
                aggsend[h, j, k] = aggregate(h, j * GROUP + k)
                return 0
            lax.fori_loop(s * PAIRS, (s + 1) * PAIRS, row, 0, unroll=True)
            agg_copy(h, j, s).start()

        def row(k, _):
            aggrecv[k, h, chip] = aggregate(h, k)
            return 0
        lax.fori_loop(s * PAIRS, (s + 1) * PAIRS, row, 0, unroll=True)

    def finish(s):
        for h in range(HALVES):
            for j in (2, 1, 3):
                agg_copy(h, j, s).wait()
        for k in range(s * PAIRS, (s + 1) * PAIRS):
            values = aggrecv[k].reshape(HALVES * CHIPS * WIDE, TILE).astype(jnp.float32)
            peak_abs = jnp.max(jnp.abs(values))
            normalized = (values / (peak_abs + epsilon)).astype(jnp.bfloat16)
            mixed = lax.dot_general(normalized, order[...], TN, preferred_element_type=jnp.float32)
            out[k * TILE:(k + 1) * TILE] = jnp.maximum(mixed + bias[...], 0.0).astype(jnp.bfloat16)

    per_step = HALF // TOTAL
    for step in range(STEPS):
        transfer(step)
        if step < TOTAL:
            body = own_row if (step + 1) * per_step <= GROUP else more_row
            lax.fori_loop(step * per_step, (step + 1) * per_step, body, 0)
        if (step + 1) * per_step == GROUP:
            for d in offsets:
                degq_copy(d).start()
        if step == TOTAL // 2:
            for d in offsets:
                degq_copy(d).wait()
            for s in range(1, feats):
                degall_copy(s).start()
            degall[feat] = degq[...]
        if step == TOTAL - 2:
            for s in range(1, feats):
                degall_copy(s).wait()
            for f in range(feats):
                for d in range(SPAN):
                    inv[pl.ds(d * ROWS + f * GROUP, GROUP)] = lax.rsqrt(degall[f, d])
            own_copy.wait()
            for n in range(CHUNKS - 2):
                scale(n)
        if step == TOTAL:
            for n in range(CHUNKS - 2, CHUNKS):
                scale(n)
        if step >= TOTAL:
            aggregate_rows(0, step - TOTAL)
    for n in range(CHUNKS, TOTAL):
        scale(n)
    for s in range(SUBS):
        aggregate_rows(1, s)
    for s in range(SUBS):
        finish(s)

    @pl.when(outer)
    def _():
        for n in range(TOTAL):
            for source in (REACH, 3, PASS, 4):
                forward(outer_sends, source, n, wait=True)

    @pl.when(inner)
    def _():
        for n in range(TOTAL):
            for source in (REACH, 1, 4, 0):
                forward(inner_sends, source, n, wait=True)


def per_device(features, tile_cols, tile_count, edge_mask, weight, bias):
    feats = lax.axis_size("feat")
    smem = pl.BlockSpec(memory_space=pltpu.SMEM)
    vmem = pl.BlockSpec(memory_space=pltpu.VMEM)
    hbm = pl.BlockSpec(memory_space=pl.ANY)
    dma = pltpu.SemaphoreType.DMA
    return pl.pallas_call(
        kernel,
        out_shape=jax.ShapeDtypeStruct((GROUP * TILE, weight.shape[1]), jnp.bfloat16),
        in_specs=[hbm, hbm, smem, smem, vmem, vmem],
        out_specs=vmem,
        scratch_shapes=[
            pltpu.VMEM((STAGES, SLOTS, TILE, TILE), jnp.int32),
            pltpu.VMEM((HALF, TILE, SLOTS * TILE), jnp.bfloat16),
            pltpu.VMEM((CORES, SPAN + 1, PART, NODES), jnp.bfloat16),
            pltpu.VMEM((HALVES, SPAN * ROWS + 1, WIDE, TILE), jnp.bfloat16),
            pltpu.VMEM((SPAN * ROWS, TILE), jnp.float32),
            pltpu.VMEM((SPAN, GROUP, TILE), jnp.float32),
            pltpu.VMEM((feats, SPAN, GROUP, TILE), jnp.float32),
            pltpu.VMEM((HALVES, CHIPS, GROUP, WIDE, TILE), jnp.bfloat16),
            pltpu.VMEM((GROUP, HALVES, CHIPS, WIDE, TILE), jnp.bfloat16),
            pltpu.VMEM(weight.shape, jnp.bfloat16),
            dma((STAGES,)), dma, dma((SPAN + 1, TOTAL)), dma((SPAN + 1, TOTAL)),
            dma((SPAN, TOTAL)), dma((SPAN, TOTAL)),
            dma((SPAN,)), dma((SPAN,)), dma((feats,)), dma((feats,)),
            dma((HALVES, CHIPS, SUBS)), dma((HALVES, CHIPS, SUBS)),
        ],
        compiler_params=pltpu.CompilerParams(
            collective_id=0, has_side_effects=True, vmem_limit_bytes=60 * 1024 * 1024),
    )(features.T, edge_mask, tile_cols.T, tile_count, weight, bias.reshape(1, -1))


def solution(mesh):
    placed = (P("blk", "feat"), P("blk", None), P("blk"), P("blk", None, None, None), P(), P())
    return jax.shard_map(
        per_device, mesh=mesh, in_specs=placed, out_specs=P(("blk", "feat"), None), check_vma=False
    )
```

```python
import functools

import jax
import jax.numpy as jnp
from jax import lax
from jax.experimental import pallas as pl
from jax.experimental.pallas import tpu as pltpu
from jax.sharding import PartitionSpec as P

MESH = pl.DeviceIdType.MESH

TILE = 128
REACH = 2
SPAN = 2 * REACH + 1
epsilon = 1e-06

CORES = 2
ROWS = 64
SLOTS = 16
PART = 32
WIDE = CORES * PART
HALF = ROWS // CORES
GROUP = 8
CHIPS = 4
STAGES = 16
NODES = ROWS * TILE

CHUNKS = 4
BLOCKS = ROWS // CHUNKS
LANES = BLOCKS * TILE
PAIRS = 2
SUBS = GROUP // PAIRS

NN = (((1,), (0,)), ((), ()))
NT = (((1,), (1,)), ((), ()))
TN = (((0,), (0,)), ((), ()))


def kernel(
    ft, mask, cols, count, weight, bias, out,
    stage, tiles, raw, scaled, inv, degq, degall, aggsend, aggrecv, picks,
    stage_sem, own_sem, panel_send, panel_recv, pair_send, pair_recv,
    degq_send, degq_recv, degall_send, degall_recv, agg_send, agg_recv,
):
    blk = lax.axis_index("blk")
    feat = lax.axis_index("feat")
    owners = lax.axis_size("blk")
    feats = lax.axis_size("feat")
    chip, core = feat // CORES, feat % CORES
    partner = (blk, chip * CORES + 1 - core)

    def owner(d):
        return lax.rem(blk + d + owners, owners)

    def block_row(q):
        j, k = q // GROUP, q % GROUP
        return lax.rem(chip + j, CHIPS) * (CORES * GROUP) + core * GROUP + k

    def stage_copy(q):
        slot = q % STAGES
        return pltpu.make_async_copy(mask.at[block_row(q)], stage.at[slot], stage_sem.at[slot])

    for q in range(STAGES):
        stage_copy(q).start()
    own_copy = pltpu.make_async_copy(ft, raw.at[core, REACH], own_sem)
    own_copy.start()

    barrier = pltpu.get_barrier_semaphore()
    offsets = [d for d in range(-REACH, REACH + 1) if d != 0]
    peers = [(owner(d), feat) for d in offsets]
    peers += [(blk, lax.rem(feat + s, feats)) for s in range(1, feats)]
    for peer in peers:
        pl.semaphore_signal(barrier, inc=1, device_id=peer, device_id_type=MESH)
    pl.semaphore_wait(barrier, len(peers))

    def piece(n):
        return pl.ds(0, PART), pl.ds(n * LANES, LANES)

    def panel_copy(d, n):
        features, nodes = piece(n)
        sign = 1 if d > 0 else -1
        target = REACH + d
        source = target - sign
        src = ft.at[features, nodes] if source == REACH else raw.at[core, source, features, nodes]
        return pltpu.make_async_remote_copy(
            src_ref=src, dst_ref=raw.at[core, target, features, nodes],
            send_sem=panel_send.at[target, n], recv_sem=panel_recv.at[target, n],
            device_id=(owner(-sign), feat), device_id_type=MESH)

    def pair_copy(slot, n):
        features, nodes = piece(n)
        here = raw.at[core, slot, features, nodes]
        return pltpu.make_async_remote_copy(
            src_ref=ft.at[features, nodes] if slot == REACH else here, dst_ref=here,
            send_sem=pair_send.at[slot, n], recv_sem=pair_recv.at[slot, n],
            device_id=partner, device_id_type=MESH)

    def relay(d, n):
        panel_copy(d, n).wait_recv()
        if abs(d) < REACH:
            panel_copy(2 * d, n).start()
        pair_copy(REACH + d, n).start()

    for n in range(CHUNKS):
        for d in (-1, 1):
            panel_copy(d, n).start()
        if n == 0:
            for m in range(CHUNKS):
                pair_copy(REACH, m).start()

    scaled[SPAN * ROWS] = jnp.zeros((WIDE, TILE), jnp.bfloat16)

    first = (blk - REACH) * ROWS
    blocks = owners * ROWS

    def convert(q):
        slot = q % STAGES
        b = block_row(q)
        used = count[b]
        for t in range(SLOTS):
            local = (cols[t, b] - first + blocks) & (blocks - 1)
            picks[q, t] = jnp.where(t < used, local, SPAN * ROWS)
        stage_copy(q).wait()
        for t in range(SLOTS):
            tiles[q, t * TILE:(t + 1) * TILE] = stage[slot, t].astype(jnp.float32).astype(jnp.bfloat16).T

    def own_row(q, _):
        convert(q)
        n = count[block_row(q)]
        total = jnp.zeros((TILE, TILE), jnp.int32)
        for t in range(SLOTS):
            total = total + stage[q, t] * (t < n).astype(jnp.int32)
        total = total.astype(jnp.float32).astype(jnp.bfloat16)
        ones = jnp.ones((8, TILE), jnp.bfloat16)
        degree = 1.0 + lax.dot_general(ones, total, NT, preferred_element_type=jnp.float32)
        degq[REACH, pl.ds(q, 1)] = degree[0:1]
        stage_copy(q + STAGES).start()
        return 0

    def more_row(q, _):
        convert(q)

        @pl.when(q < HALF - STAGES)
        def _():
            stage_copy(q + STAGES).start()
        return 0

    def degq_copy(d):
        return pltpu.make_async_remote_copy(
            src_ref=degq.at[REACH], dst_ref=degq.at[REACH - d],
            send_sem=degq_send.at[REACH - d], recv_sem=degq_recv.at[REACH - d],
            device_id=(owner(d), feat), device_id_type=MESH)

    def degall_copy(s):
        return pltpu.make_async_remote_copy(
            src_ref=degq, dst_ref=degall.at[feat],
            send_sem=degall_send.at[s], recv_sem=degall_recv.at[s],
            device_id=(blk, lax.rem(feat + s, feats)), device_id_type=MESH)

    def scale(n, *ds):
        for d in ds:
            pair_copy(REACH + d, n).wait()
        for d in ds:
            slot = REACH + d

            def body(i, _, slot=slot):
                block = n * BLOCKS + i
                nodes = pl.ds(pl.multiple_of(block * TILE, TILE), TILE)
                factor = inv[pl.ds(slot * ROWS + block, 1)]
                for k in range(CORES):
                    values = raw[k, slot, :, nodes].astype(jnp.float32)
                    scaled[slot * ROWS + block, k * PART:(k + 1) * PART] = (values * factor).astype(jnp.bfloat16)
                return 0
            lax.fori_loop(0, BLOCKS, body, 0, unroll=4)

    def agg_copy(j, s):
        rows = pl.ds(s * PAIRS, PAIRS)
        return pltpu.make_async_remote_copy(
            src_ref=aggsend.at[j, rows], dst_ref=aggrecv.at[rows, chip],
            send_sem=agg_send.at[j, s], recv_sem=agg_recv.at[j, s],
            device_id=(blk, lax.rem(chip + j, CHIPS) * CORES + core), device_id_type=MESH)

    def aggregate_rows(s):
        def row(i, _):
            j, k = i // PAIRS, s * PAIRS + i % PAIRS
            q = j * GROUP + k
            b = block_row(q)
            left = jnp.concatenate([scaled[picks[q, t]] for t in range(SLOTS)], axis=1)
            total = lax.dot_general(left, tiles[q], NN, preferred_element_type=jnp.float32)
            total = total + scaled[REACH * ROWS + b].astype(jnp.float32)
            aggsend[j, k] = (total * inv[pl.ds(REACH * ROWS + b, 1)]).astype(jnp.bfloat16)
            return 0
        lax.fori_loop(0, CHIPS * PAIRS, row, 0, unroll=4)
        for j in (2, 1, 3):
            agg_copy(j, s).start()
        rows = pl.ds(s * PAIRS, PAIRS)
        aggrecv[rows, chip] = aggsend[0, rows]

    def finish(s):
        for j in (2, 1, 3):
            agg_copy(j, s).wait()
        for k in range(s * PAIRS, (s + 1) * PAIRS):
            values = aggrecv[k].reshape(CHIPS * WIDE, TILE).astype(jnp.float32)
            peak_abs = jnp.max(jnp.abs(values))
            normalized = (values / (peak_abs + epsilon)).astype(jnp.bfloat16)
            mixed = lax.dot_general(normalized, weight[...], TN, preferred_element_type=jnp.float32)
            out[k * TILE:(k + 1) * TILE] = jnp.maximum(mixed + bias[...], 0.0).astype(jnp.bfloat16)

    def near(n):
        for d in (-1, 1):
            relay(d, n)

    lax.fori_loop(0, GROUP, own_row, 0)
    for d in offsets:
        degq_copy(d).start()
    lax.fori_loop(GROUP, 12, more_row, 0)
    near(0)
    lax.fori_loop(12, 15, more_row, 0)
    for d in offsets:
        degq_copy(d).wait()
    for s in range(1, feats):
        degall_copy(s).start()
    degall[feat] = degq[...]
    lax.fori_loop(15, 19, more_row, 0)
    near(1)
    lax.fori_loop(19, 26, more_row, 0)
    near(2)
    lax.fori_loop(26, HALF, more_row, 0)
    near(3)
    for s in range(1, feats):
        degall_copy(s).wait()
    for f in range(feats):
        for d in range(SPAN):
            inv[pl.ds(d * ROWS + f * GROUP, GROUP)] = lax.rsqrt(degall[f, d])
    own_copy.wait()
    for n in range(CHUNKS):
        scale(n, 0, -1, 1)
        for d in (-2, 2):
            relay(d, n)
        if n > 0:
            scale(n - 1, -2, 2)
    scale(CHUNKS - 1, -2, 2)
    for s in range(SUBS):
        aggregate_rows(s)
        if s >= 2:
            finish(s - 2)
    for s in (SUBS - 2, SUBS - 1):
        finish(s)
    for n in range(CHUNKS):
        for d in offsets:
            panel_copy(d, n).wait_send()


def per_device(features, tile_cols, tile_count, edge_mask, weight, bias):
    feats = lax.axis_size("feat")
    smem = pl.BlockSpec(memory_space=pltpu.SMEM)
    vmem = pl.BlockSpec(memory_space=pltpu.VMEM)
    hbm = pl.BlockSpec(memory_space=pl.ANY)
    dma = pltpu.SemaphoreType.DMA
    return pl.pallas_call(
        kernel,
        out_shape=jax.ShapeDtypeStruct((GROUP * TILE, weight.shape[1]), jnp.bfloat16),
        in_specs=[hbm, hbm, smem, smem, vmem, vmem],
        out_specs=vmem,
        scratch_shapes=[
            pltpu.VMEM((STAGES, SLOTS, TILE, TILE), jnp.int32),
            pltpu.VMEM((HALF, SLOTS * TILE, TILE), jnp.bfloat16),
            pltpu.VMEM((CORES, SPAN, PART, NODES), jnp.bfloat16),
            pltpu.VMEM((SPAN * ROWS + 1, WIDE, TILE), jnp.bfloat16),
            pltpu.VMEM((SPAN * ROWS, TILE), jnp.float32),
            pltpu.VMEM((SPAN, GROUP, TILE), jnp.float32),
            pltpu.VMEM((feats, SPAN, GROUP, TILE), jnp.float32),
            pltpu.VMEM((CHIPS, GROUP, WIDE, TILE), jnp.bfloat16),
            pltpu.VMEM((GROUP, CHIPS, WIDE, TILE), jnp.bfloat16),
            pltpu.SMEM((HALF, SLOTS), jnp.int32),
            dma((STAGES,)), dma, dma((SPAN, CHUNKS)), dma((SPAN, CHUNKS)),
            dma((SPAN, CHUNKS)), dma((SPAN, CHUNKS)),
            dma((SPAN,)), dma((SPAN,)), dma((feats,)), dma((feats,)),
            dma((CHIPS, SUBS)), dma((CHIPS, SUBS)),
        ],
        compiler_params=pltpu.CompilerParams(
            collective_id=0, has_side_effects=True, vmem_limit_bytes=60 * 1024 * 1024),
    )(features.T, edge_mask, tile_cols.T, tile_count, weight, bias.reshape(1, -1))


def solution(mesh):
    placed = (P("blk", "feat"), P("blk", None), P("blk"), P("blk", None, None, None), P(), P())
    return jax.shard_map(
        per_device, mesh=mesh, in_specs=placed, out_specs=P(("blk", "feat"), None), check_vma=False
    )
```

```python
import functools

import jax
import jax.numpy as jnp
from jax import lax
from jax.experimental import pallas as pl
from jax.experimental.pallas import tpu as pltpu
from jax.sharding import PartitionSpec as P

MESH = pl.DeviceIdType.MESH

TILE = 128
REACH = 2
SPAN = 2 * REACH + 1
epsilon = 1e-06

CORES = 2
ROWS = 64
SLOTS = 16
PART = 32
HALVES = 2
SUB = PART // HALVES
WIDE = CORES * SUB
HALF = ROWS // CORES
GROUP = 8
CHIPS = 4
STAGES = 16
DEGREES = 1
NODES = ROWS * TILE

CUTS = 2
CHUNKS = HALVES * CUTS
BLOCKS = ROWS // CUTS
LANES = BLOCKS * TILE
AHEAD = 4
PAIRS = 2
SUBS = GROUP // PAIRS

NN = (((1,), (0,)), ((), ()))
NT = (((1,), (1,)), ((), ()))
TN = (((0,), (0,)), ((), ()))


def kernel(
    ft, mask, cols_in, count_in, weight_in, bias_in, out_hbm,
    cols, count, weight, bias, out, stage, tiles, raw, scaled, inv, degq, degall, aggsend, aggrecv, picks, order,
    small_sem, out_sem, stage_sem, own_sem, panel_send, panel_recv, pair_send, pair_recv,
    degq_send, degq_recv, degall_send, degall_recv, agg_send, agg_recv,
):
    blk = lax.axis_index("blk")
    feat = lax.axis_index("feat")
    owners = lax.axis_size("blk")
    feats = lax.axis_size("feat")
    chip, core = feat // CORES, feat % CORES
    partner = (blk, chip * CORES + 1 - core)

    def owner(d):
        return lax.rem(blk + d + owners, owners)

    def block_row(q):
        j, k = q // GROUP, q % GROUP
        return lax.rem(chip + j, CHIPS) * (CORES * GROUP) + core * GROUP + k

    def stage_copy(q):
        slot = q % STAGES
        return pltpu.make_async_copy(mask.at[block_row(q)], stage.at[slot], stage_sem.at[slot])

    barrier = pltpu.get_barrier_semaphore()
    offsets = [d for d in range(-REACH, REACH + 1) if d != 0]
    peers = [(owner(d), feat) for d in offsets]
    peers += [(blk, lax.rem(feat + s, feats)) for s in range(1, feats)]
    for peer in peers:
        pl.semaphore_signal(barrier, inc=1, device_id=peer, device_id_type=MESH)
    small = [
        pltpu.make_async_copy(source, target, small_sem.at[i]) for i, (source, target) in enumerate(
            ((cols_in, cols), (count_in, count), (weight_in, weight), (bias_in, bias)))]
    for copy in small[:2]:
        copy.start()
    for q in range(STAGES):
        stage_copy(q).start()
    own_copy = pltpu.make_async_copy(ft, raw.at[core, REACH], own_sem)
    own_copy.start()
    for copy in small[2:]:
        copy.start()
    for copy in small[:2]:
        copy.wait()
    pl.semaphore_wait(barrier, len(peers))

    def piece(n):
        return pl.ds(n // CUTS * SUB, SUB), pl.ds(n % CUTS * LANES, LANES)

    def panel_copy(d, n):
        features, nodes = piece(n)
        sign = 1 if d > 0 else -1
        target = REACH + d
        source = target - sign
        src = ft.at[features, nodes] if source == REACH else raw.at[core, source, features, nodes]
        return pltpu.make_async_remote_copy(
            src_ref=src, dst_ref=raw.at[core, target, features, nodes],
            send_sem=panel_send.at[target, n], recv_sem=panel_recv.at[target, n],
            device_id=(owner(-sign), feat), device_id_type=MESH)

    def pair_copy(slot, n):
        features, nodes = piece(n)
        here = raw.at[core, slot, features, nodes]
        return pltpu.make_async_remote_copy(
            src_ref=ft.at[features, nodes] if slot == REACH else here, dst_ref=here,
            send_sem=pair_send.at[slot, n], recv_sem=pair_recv.at[slot, n],
            device_id=partner, device_id_type=MESH)

    def relay(d, n):
        panel_copy(d, n).wait_recv()
        if abs(d) < REACH:
            panel_copy(2 * d, n).start()
        pair_copy(REACH + d, n).start()

    def send_own(n):
        for d in (-1, 1):
            panel_copy(d, n).start()

    for n in range(AHEAD):
        send_own(n)
    for n in range(CHUNKS):
        pair_copy(REACH, n).start()

    for h in range(HALVES):
        scaled[h, SPAN * ROWS] = jnp.zeros((WIDE, TILE), jnp.bfloat16)

    first = (blk - REACH) * ROWS
    blocks = owners * ROWS

    def convert(q):
        slot = q % STAGES
        b = block_row(q)
        used = count[b]
        for t in range(SLOTS):
            local = (cols[t, b] - first + blocks) & (blocks - 1)
            picks[q, t] = jnp.where(t < used, local, SPAN * ROWS)
        stage_copy(q).wait()
        for t in range(SLOTS):
            tiles[q, t * TILE:(t + 1) * TILE] = stage[slot, t].astype(jnp.float32).astype(jnp.bfloat16).T

    def own_row(q, _):
        convert(q)
        n = count[block_row(q)]
        total = jnp.zeros((TILE, TILE), jnp.int32)
        for t in range(SLOTS):
            total = total + stage[q, t] * (t < n).astype(jnp.int32)
        total = total.astype(jnp.float32).astype(jnp.bfloat16)
        ones = jnp.ones((8, TILE), jnp.bfloat16)
        degree = 1.0 + lax.dot_general(ones, total, NT, preferred_element_type=jnp.float32)
        degq[REACH, pl.ds(q, 1)] = degree[0:1]
        stage_copy(q + STAGES).start()
        return 0

    def more_row(q, _):
        convert(q)

        @pl.when(q < HALF - STAGES)
        def _():
            stage_copy(q + STAGES).start()
        return 0

    def degq_copy(d):
        return pltpu.make_async_remote_copy(
            src_ref=degq.at[REACH], dst_ref=degq.at[REACH - d],
            send_sem=degq_send.at[REACH - d], recv_sem=degq_recv.at[REACH - d],
            device_id=(owner(d), feat), device_id_type=MESH)

    def degall_copy(s):
        return pltpu.make_async_remote_copy(
            src_ref=degq, dst_ref=degall.at[feat],
            send_sem=degall_send.at[s], recv_sem=degall_recv.at[s],
            device_id=(blk, lax.rem(feat + s, feats)), device_id_type=MESH)

    def scale(n, *ds):
        h = n // CUTS
        for d in ds:
            pair_copy(REACH + d, n).wait()
        for d in ds:
            slot = REACH + d

            def body(i, _, slot=slot):
                block = n % CUTS * BLOCKS + i
                nodes = pl.ds(pl.multiple_of(block * TILE, TILE), TILE)
                factor = inv[pl.ds(slot * ROWS + block, 1)]
                for k in range(CORES):
                    values = raw[k, slot, h * SUB:(h + 1) * SUB, nodes].astype(jnp.float32)
                    scaled[h, slot * ROWS + block, k * SUB:(k + 1) * SUB] = (values * factor).astype(jnp.bfloat16)
                return 0
            lax.fori_loop(0, BLOCKS, body, 0, unroll=4)

    def agg_copy(h, j, s):
        rows = pl.ds(s * PAIRS, PAIRS)
        return pltpu.make_async_remote_copy(
            src_ref=aggsend.at[h, j, rows], dst_ref=aggrecv.at[rows, h, chip],
            send_sem=agg_send.at[h, j, s], recv_sem=agg_recv.at[h, j, s],
            device_id=(blk, lax.rem(chip + j, CHIPS) * CORES + core), device_id_type=MESH)

    def aggregate_rows(h, s):
        def row(i, _):
            j, k = i // PAIRS, s * PAIRS + i % PAIRS
            q = j * GROUP + k
            b = block_row(q)
            left = jnp.concatenate([scaled[h, picks[q, t]] for t in range(SLOTS)], axis=1)
            total = lax.dot_general(left, tiles[q], NN, preferred_element_type=jnp.float32)
            total = total + scaled[h, REACH * ROWS + b].astype(jnp.float32)
            aggsend[h, j, k] = (total * inv[pl.ds(REACH * ROWS + b, 1)]).astype(jnp.bfloat16)
            return 0
        lax.fori_loop(0, CHIPS * PAIRS, row, 0, unroll=8)
        for j in (2, 1, 3):
            agg_copy(h, j, s).start()
        rows = pl.ds(s * PAIRS, PAIRS)
        aggrecv[rows, h, chip] = aggsend[h, 0, rows]

    def out_copy(s):
        rows = pl.ds(s * PAIRS * TILE, PAIRS * TILE)
        return pltpu.make_async_copy(out.at[rows], out_hbm.at[rows], out_sem.at[s])

    def finish(s):
        for h in range(HALVES):
            for j in (2, 1, 3):
                agg_copy(h, j, s).wait()
        for k in range(s * PAIRS, (s + 1) * PAIRS):
            values = aggrecv[k].reshape(HALVES * CHIPS * WIDE, TILE).astype(jnp.float32)
            peak_abs = jnp.max(jnp.abs(values))
            normalized = (values / (peak_abs + epsilon)).astype(jnp.bfloat16)
            mixed = lax.dot_general(normalized, order[...], TN, preferred_element_type=jnp.float32)
            out[k * TILE:(k + 1) * TILE] = jnp.maximum(mixed + bias[...], 0.0).astype(jnp.bfloat16)

    def near(n):
        for d in (-1, 1):
            relay(d, n)
        if n + AHEAD < CHUNKS:
            send_own(n + AHEAD)

    def far(n):
        for d in (-2, 2):
            relay(d, n)

    lax.fori_loop(0, GROUP, own_row, 0)
    for d in offsets:
        degq_copy(d).start()
    done = GROUP
    for n in range(CHUNKS):
        near(n)
        if n == DEGREES:
            for d in offsets:
                degq_copy(d).wait()
            for s in range(1, feats):
                degall_copy(s).start()
            degall[feat] = degq[...]
        more = (HALF - GROUP) * (n + 1) // CHUNKS + GROUP
        lax.fori_loop(done, more, more_row, 0)
        done = more
    far(0)
    for s in range(1, feats):
        degall_copy(s).wait()
    for f in range(feats):
        for d in range(SPAN):
            inv[pl.ds(d * ROWS + f * GROUP, GROUP)] = lax.rsqrt(degall[f, d])
    own_copy.wait()
    scale(0, 0, -1, 1)
    far(1)
    scale(1, 0, -1, 1)
    scale(0, -2, 2)
    scale(1, -2, 2)
    aggregate_rows(0, 0)
    scale(2, 0, -1, 1)
    aggregate_rows(0, 1)
    far(2)
    scale(3, 0, -1, 1)
    aggregate_rows(0, 2)
    scale(2, -2, 2)
    for copy in small[2:]:
        copy.wait()
    for x in range(CHIPS):
        for c in range(CORES):
            for h in range(HALVES):
                source = (x * CORES + c) * PART + h * SUB
                target = (h * CHIPS + x) * WIDE + c * SUB
                order[target:target + SUB] = weight[source:source + SUB]
    aggregate_rows(0, 3)
    far(3)
    scale(3, -2, 2)
    for s in range(SUBS):
        aggregate_rows(1, s)
        if s >= 2:
            finish(s - 2)
            out_copy(s - 2).start()
    for s in (SUBS - 2, SUBS - 1):
        finish(s)
        out_copy(s).start()
    for n in range(CHUNKS):
        for d in offsets:
            panel_copy(d, n).wait_send()
    for s in range(SUBS):
        out_copy(s).wait()


def per_device(features, tile_cols, tile_count, edge_mask, weight, bias):
    feats = lax.axis_size("feat")
    hbm = pl.BlockSpec(memory_space=pl.ANY)
    dma = pltpu.SemaphoreType.DMA
    return pl.pallas_call(
        kernel,
        out_shape=jax.ShapeDtypeStruct((GROUP * TILE, weight.shape[1]), jnp.bfloat16),
        in_specs=[hbm] * 6,
        out_specs=hbm,
        scratch_shapes=[
            pltpu.SMEM((SLOTS, ROWS), jnp.int32),
            pltpu.SMEM((ROWS,), jnp.int32),
            pltpu.VMEM(weight.shape, jnp.bfloat16),
            pltpu.VMEM((1, weight.shape[1]), jnp.float32),
            pltpu.VMEM((GROUP * TILE, weight.shape[1]), jnp.bfloat16),
            pltpu.VMEM((STAGES, SLOTS, TILE, TILE), jnp.int32),
            pltpu.VMEM((HALF, SLOTS * TILE, TILE), jnp.bfloat16),
            pltpu.VMEM((CORES, SPAN, PART, NODES), jnp.bfloat16),
            pltpu.VMEM((HALVES, SPAN * ROWS + 1, WIDE, TILE), jnp.bfloat16),
            pltpu.VMEM((SPAN * ROWS, TILE), jnp.float32),
            pltpu.VMEM((SPAN, GROUP, TILE), jnp.float32),
            pltpu.VMEM((feats, SPAN, GROUP, TILE), jnp.float32),
            pltpu.VMEM((HALVES, CHIPS, GROUP, WIDE, TILE), jnp.bfloat16),
            pltpu.VMEM((GROUP, HALVES, CHIPS, WIDE, TILE), jnp.bfloat16),
            pltpu.SMEM((HALF, SLOTS), jnp.int32),
            pltpu.VMEM(weight.shape, jnp.bfloat16),
            dma((4,)), dma((SUBS,)), dma((STAGES,)), dma, dma((SPAN, CHUNKS)), dma((SPAN, CHUNKS)),
            dma((SPAN, CHUNKS)), dma((SPAN, CHUNKS)),
            dma((SPAN,)), dma((SPAN,)), dma((feats,)), dma((feats,)),
            dma((HALVES, CHIPS, SUBS)), dma((HALVES, CHIPS, SUBS)),
        ],
        compiler_params=pltpu.CompilerParams(
            collective_id=0, has_side_effects=True, vmem_limit_bytes=60 * 1024 * 1024),
    )(features.T, edge_mask, tile_cols.T, tile_count, weight, bias.reshape(1, -1))


def solution(mesh):
    placed = (P("blk", "feat"), P("blk", None), P("blk"), P("blk", None, None, None), P(), P())
    return jax.shard_map(
        per_device, mesh=mesh, in_specs=placed, out_specs=P(("blk", "feat"), None), check_vma=False
    )
```

```python
import functools

import jax
import jax.numpy as jnp
from jax import lax
from jax.experimental import pallas as pl
from jax.experimental.pallas import tpu as pltpu
from jax.sharding import PartitionSpec as P

MESH = pl.DeviceIdType.MESH

TILE = 128
REACH = 2
SPAN = 2 * REACH + 1
epsilon = 1e-06

CORES = 2
ROWS = 64
SLOTS = 16
PART = 32
HALVES = 2
SUB = PART // HALVES
WIDE = CORES * SUB
HALF = ROWS // CORES
GROUP = 8
CHIPS = 4
STAGES = 8
DEGREES = 1
NODES = ROWS * TILE

CUTS = 2
CHUNKS = HALVES * CUTS
BLOCKS = ROWS // CUTS
LANES = BLOCKS * TILE
AHEAD = 4
PAIRS = 2
SUBS = GROUP // PAIRS

NN = (((1,), (0,)), ((), ()))
NT = (((1,), (1,)), ((), ()))
TN = (((0,), (0,)), ((), ()))


def kernel(
    ft, mask, cols_in, count_in, weight_in, bias_in, out_hbm,
    cols, count, weight, bias, out, stage, tiles, raw, scaled, inv, degq, degall, aggsend, aggrecv, picks, order,
    small_sem, out_sem, stage_sem, own_sem, panel_send, panel_recv, pair_send, pair_recv,
    degq_send, degq_recv, degall_send, degall_recv, agg_send, agg_recv,
):
    blk = lax.axis_index("blk")
    feat = lax.axis_index("feat")
    owners = lax.axis_size("blk")
    feats = lax.axis_size("feat")
    chip, core = feat // CORES, feat % CORES
    partner = (blk, chip * CORES + 1 - core)

    def owner(d):
        return lax.rem(blk + d + owners, owners)

    def block_row(q):
        j, k = q // GROUP, q % GROUP
        return lax.rem(chip + j, CHIPS) * (CORES * GROUP) + core * GROUP + k

    def stage_copy(q):
        slot = q % STAGES
        return pltpu.make_async_copy(mask.at[block_row(q)], stage.at[slot], stage_sem.at[slot])

    barrier = pltpu.get_barrier_semaphore()
    offsets = [d for d in range(-REACH, REACH + 1) if d != 0]
    peers = [(owner(d), feat) for d in offsets]
    peers += [(blk, lax.rem(feat + s, feats)) for s in range(1, feats)]
    for peer in peers:
        pl.semaphore_signal(barrier, inc=1, device_id=peer, device_id_type=MESH)
    small = [
        pltpu.make_async_copy(source, target, small_sem.at[i]) for i, (source, target) in enumerate(
            ((cols_in, cols), (count_in, count), (weight_in, weight), (bias_in, bias)))]
    for copy in small[:2]:
        copy.start()
    for q in range(STAGES):
        stage_copy(q).start()
    own_copy = pltpu.make_async_copy(ft, raw.at[core, REACH], own_sem)
    own_copy.start()
    for copy in small[2:]:
        copy.start()
    for copy in small[:2]:
        copy.wait()
    pl.semaphore_wait(barrier, len(peers))

    def piece(n):
        return pl.ds(n // CUTS * SUB, SUB), pl.ds(n % CUTS * LANES, LANES)

    def panel_copy(d, n):
        features, nodes = piece(n)
        sign = 1 if d > 0 else -1
        target = REACH + d
        source = target - sign
        src = ft.at[features, nodes] if source == REACH else raw.at[core, source, features, nodes]
        return pltpu.make_async_remote_copy(
            src_ref=src, dst_ref=raw.at[core, target, features, nodes],
            send_sem=panel_send.at[target, n], recv_sem=panel_recv.at[target, n],
            device_id=(owner(-sign), feat), device_id_type=MESH)

    def pair_copy(slot, n):
        features, nodes = piece(n)
        here = raw.at[core, slot, features, nodes]
        return pltpu.make_async_remote_copy(
            src_ref=ft.at[features, nodes] if slot == REACH else here, dst_ref=here,
            send_sem=pair_send.at[slot, n], recv_sem=pair_recv.at[slot, n],
            device_id=partner, device_id_type=MESH)

    def relay(d, n):
        panel_copy(d, n).wait_recv()
        if abs(d) < REACH:
            panel_copy(2 * d, n).start()
        pair_copy(REACH + d, n).start()

    def send_own(n):
        for d in (-1, 1):
            panel_copy(d, n).start()

    for n in range(AHEAD):
        send_own(n)
    for n in range(CHUNKS):
        pair_copy(REACH, n).start()

    for h in range(HALVES):
        scaled[h, SPAN * ROWS] = jnp.zeros((WIDE, TILE), jnp.bfloat16)

    first = (blk - REACH) * ROWS
    blocks = owners * ROWS

    def convert(q):
        slot = q % STAGES
        b = block_row(q)
        used = count[b]
        for t in range(SLOTS):
            local = (cols[t, b] - first + blocks) & (blocks - 1)
            picks[q, t] = jnp.where(t < used, local, SPAN * ROWS)
        stage_copy(q).wait()
        for t in range(SLOTS):
            tiles[q, t * TILE:(t + 1) * TILE] = stage[slot, t].astype(jnp.float32).astype(jnp.bfloat16).T

    def own_row(q, _):
        convert(q)
        n = count[block_row(q)]
        total = jnp.zeros((TILE, TILE), jnp.int32)
        for t in range(SLOTS):
            total = total + stage[q, t] * (t < n).astype(jnp.int32)
        total = total.astype(jnp.float32).astype(jnp.bfloat16)
        ones = jnp.ones((8, TILE), jnp.bfloat16)
        degree = 1.0 + lax.dot_general(ones, total, NT, preferred_element_type=jnp.float32)
        degq[REACH, pl.ds(q, 1)] = degree[0:1]
        stage_copy(q + STAGES).start()
        return 0

    def more_row(q, _):
        convert(q)

        @pl.when(q < HALF - STAGES)
        def _():
            stage_copy(q + STAGES).start()
        return 0

    def degq_copy(d):
        return pltpu.make_async_remote_copy(
            src_ref=degq.at[REACH], dst_ref=degq.at[REACH - d],
            send_sem=degq_send.at[REACH - d], recv_sem=degq_recv.at[REACH - d],
            device_id=(owner(d), feat), device_id_type=MESH)

    def degall_copy(s):
        return pltpu.make_async_remote_copy(
            src_ref=degq, dst_ref=degall.at[feat],
            send_sem=degall_send.at[s], recv_sem=degall_recv.at[s],
            device_id=(blk, lax.rem(feat + s, feats)), device_id_type=MESH)

    def scale(n, *ds):
        h = n // CUTS
        for d in ds:
            pair_copy(REACH + d, n).wait()
        for d in ds:
            slot = REACH + d

            def body(i, _, slot=slot):
                block = n % CUTS * BLOCKS + i
                nodes = pl.ds(pl.multiple_of(block * TILE, TILE), TILE)
                factor = inv[pl.ds(slot * ROWS + block, 1)]
                for k in range(CORES):
                    values = raw[k, slot, h * SUB:(h + 1) * SUB, nodes].astype(jnp.float32)
                    scaled[h, slot * ROWS + block, k * SUB:(k + 1) * SUB] = (values * factor).astype(jnp.bfloat16)
                return 0
            lax.fori_loop(0, BLOCKS, body, 0, unroll=4)

    def agg_copy(h, j, s):
        rows = pl.ds(s * PAIRS, PAIRS)
        return pltpu.make_async_remote_copy(
            src_ref=aggsend.at[h, j, rows], dst_ref=aggrecv.at[rows, h, chip],
            send_sem=agg_send.at[h, j, s], recv_sem=agg_recv.at[h, j, s],
            device_id=(blk, lax.rem(chip + j, CHIPS) * CORES + core), device_id_type=MESH)

    def aggregate_rows(h, s):
        def row(i, _):
            j, k = i // PAIRS, s * PAIRS + i % PAIRS
            q = j * GROUP + k
            b = block_row(q)
            left = jnp.concatenate([scaled[h, picks[q, t]] for t in range(SLOTS)], axis=1)
            total = lax.dot_general(left, tiles[q], NN, preferred_element_type=jnp.float32)
            total = total + scaled[h, REACH * ROWS + b].astype(jnp.float32)
            aggsend[h, j, k] = (total * inv[pl.ds(REACH * ROWS + b, 1)]).astype(jnp.bfloat16)
            return 0
        lax.fori_loop(PAIRS, CHIPS * PAIRS, row, 0, unroll=True)
        for j in (2, 1, 3):
            agg_copy(h, j, s).start()
        lax.fori_loop(0, PAIRS, row, 0, unroll=True)
        rows = pl.ds(s * PAIRS, PAIRS)
        aggrecv[rows, h, chip] = aggsend[h, 0, rows]

    def out_copy(s):
        rows = pl.ds(s * PAIRS * TILE, PAIRS * TILE)
        return pltpu.make_async_copy(out.at[rows], out_hbm.at[rows], out_sem.at[s])

    def finish(s):
        for h in range(HALVES):
            for j in (2, 1, 3):
                agg_copy(h, j, s).wait()
        for k in range(s * PAIRS, (s + 1) * PAIRS):
            values = aggrecv[k].reshape(HALVES * CHIPS * WIDE, TILE).astype(jnp.float32)
            peak_abs = jnp.max(jnp.abs(values))
            normalized = (values / (peak_abs + epsilon)).astype(jnp.bfloat16)
            mixed = lax.dot_general(normalized, order[...], TN, preferred_element_type=jnp.float32)
            out[k * TILE:(k + 1) * TILE] = jnp.maximum(mixed + bias[...], 0.0).astype(jnp.bfloat16)

    def near(n):
        for d in (-1, 1):
            relay(d, n)
        if n + AHEAD < CHUNKS:
            send_own(n + AHEAD)

    def far(n):
        for d in (-2, 2):
            relay(d, n)

    lax.fori_loop(0, GROUP, own_row, 0)
    for d in offsets:
        degq_copy(d).start()
    done = GROUP
    for n in range(CHUNKS):
        near(n)
        if n == DEGREES:
            for d in offsets:
                degq_copy(d).wait()
            for s in range(1, feats):
                degall_copy(s).start()
            degall[feat] = degq[...]
        more = (HALF - GROUP) * (n + 1) // CHUNKS + GROUP
        lax.fori_loop(done, more, more_row, 0)
        done = more
    far(0)
    for s in range(1, feats):
        degall_copy(s).wait()
    for f in range(feats):
        for d in range(SPAN):
            inv[pl.ds(d * ROWS + f * GROUP, GROUP)] = lax.rsqrt(degall[f, d])
    own_copy.wait()
    scale(0, 0, -1, 1)
    far(1)
    scale(1, 0, -1, 1)
    scale(0, -2, 2)
    scale(1, -2, 2)
    aggregate_rows(0, 0)
    scale(2, 0, -1, 1)
    aggregate_rows(0, 1)
    far(2)
    scale(3, 0, -1, 1)
    aggregate_rows(0, 2)
    scale(2, -2, 2)
    for copy in small[2:]:
        copy.wait()
    for x in range(CHIPS):
        for c in range(CORES):
            for h in range(HALVES):
                source = (x * CORES + c) * PART + h * SUB
                target = (h * CHIPS + x) * WIDE + c * SUB
                order[target:target + SUB] = weight[source:source + SUB]
    far(3)
    aggregate_rows(0, 3)
    scale(3, -2, 2)
    for s in range(SUBS):
        aggregate_rows(1, s)
        if s >= 2:
            finish(s - 2)
            out_copy(s - 2).start()
    for s in (SUBS - 2, SUBS - 1):
        finish(s)
        out_copy(s).start()
    for n in range(CHUNKS):
        for d in offsets:
            panel_copy(d, n).wait_send()
    for s in range(SUBS):
        out_copy(s).wait()


def per_device(features, tile_cols, tile_count, edge_mask, weight, bias):
    feats = lax.axis_size("feat")
    hbm = pl.BlockSpec(memory_space=pl.ANY)
    dma = pltpu.SemaphoreType.DMA
    return pl.pallas_call(
        kernel,
        out_shape=jax.ShapeDtypeStruct((GROUP * TILE, weight.shape[1]), jnp.bfloat16),
        in_specs=[hbm] * 6,
        out_specs=hbm,
        scratch_shapes=[
            pltpu.SMEM((SLOTS, ROWS), jnp.int32),
            pltpu.SMEM((ROWS,), jnp.int32),
            pltpu.VMEM(weight.shape, jnp.bfloat16),
            pltpu.VMEM((1, weight.shape[1]), jnp.float32),
            pltpu.VMEM((GROUP * TILE, weight.shape[1]), jnp.bfloat16),
            pltpu.VMEM((STAGES, SLOTS, TILE, TILE), jnp.int32),
            pltpu.VMEM((HALF, SLOTS * TILE, TILE), jnp.bfloat16),
            pltpu.VMEM((CORES, SPAN, PART, NODES), jnp.bfloat16),
            pltpu.VMEM((HALVES, SPAN * ROWS + 1, WIDE, TILE), jnp.bfloat16),
            pltpu.VMEM((SPAN * ROWS, TILE), jnp.float32),
            pltpu.VMEM((SPAN, GROUP, TILE), jnp.float32),
            pltpu.VMEM((feats, SPAN, GROUP, TILE), jnp.float32),
            pltpu.VMEM((HALVES, CHIPS, GROUP, WIDE, TILE), jnp.bfloat16),
            pltpu.VMEM((GROUP, HALVES, CHIPS, WIDE, TILE), jnp.bfloat16),
            pltpu.SMEM((HALF, SLOTS), jnp.int32),
            pltpu.VMEM(weight.shape, jnp.bfloat16),
            dma((4,)), dma((SUBS,)), dma((STAGES,)), dma, dma((SPAN, CHUNKS)), dma((SPAN, CHUNKS)),
            dma((SPAN, CHUNKS)), dma((SPAN, CHUNKS)),
            dma((SPAN,)), dma((SPAN,)), dma((feats,)), dma((feats,)),
            dma((HALVES, CHIPS, SUBS)), dma((HALVES, CHIPS, SUBS)),
        ],
        compiler_params=pltpu.CompilerParams(
            collective_id=0, has_side_effects=True, vmem_limit_bytes=60 * 1024 * 1024),
    )(features.T, edge_mask, tile_cols.T, tile_count, weight, bias.reshape(1, -1))


def solution(mesh):
    placed = (P("blk", "feat"), P("blk", None), P("blk"), P("blk", None, None, None), P(), P())
    return jax.shard_map(
        per_device, mesh=mesh, in_specs=placed, out_specs=P(("blk", "feat"), None), check_vma=False
    )
```

```python
import functools

import jax
import jax.numpy as jnp
from jax import lax
from jax.experimental import pallas as pl
from jax.experimental.pallas import tpu as pltpu
from jax.sharding import PartitionSpec as P

MESH = pl.DeviceIdType.MESH

TILE = 128
REACH = 2
SPAN = 2 * REACH + 1
epsilon = 1e-06

CORES = 2
ROWS = 64
SLOTS = 16
PART = 32
HALVES = 2
SUB = PART // HALVES
WIDE = CORES * SUB
HALF = ROWS // CORES
GROUP = 8
CHIPS = 4
STAGES = 8
DEGREES = 1
NODES = ROWS * TILE

CUTS = 2
CHUNKS = HALVES * CUTS
BLOCKS = ROWS // CUTS
LANES = BLOCKS * TILE
AHEAD = 4
PAIRS = 2
SUBS = GROUP // PAIRS

NN = (((1,), (0,)), ((), ()))
NT = (((1,), (1,)), ((), ()))
TN = (((0,), (0,)), ((), ()))


def kernel(
    ft, mask, cols_in, count_in, weight_in, bias_in, out_hbm,
    cols, count, weight, bias, out, stage, tiles, raw, scaled, inv, degq, degall, aggsend, aggrecv, picks, order,
    small_sem, out_sem, stage_sem, own_sem, panel_send, panel_recv, pair_send, pair_recv,
    degq_send, degq_recv, degall_send, degall_recv, agg_send, agg_recv,
):
    blk = lax.axis_index("blk")
    feat = lax.axis_index("feat")
    owners = lax.axis_size("blk")
    feats = lax.axis_size("feat")
    chip, core = feat // CORES, feat % CORES
    partner = (blk, chip * CORES + 1 - core)

    def owner(d):
        return lax.rem(blk + d + owners, owners)

    def block_row(q):
        j, k = q // GROUP, q % GROUP
        return lax.rem(chip + j, CHIPS) * (CORES * GROUP) + core * GROUP + k

    def stage_copy(q):
        slot = q % STAGES
        return pltpu.make_async_copy(mask.at[block_row(q)], stage.at[slot], stage_sem.at[slot])

    barrier = pltpu.get_barrier_semaphore()
    offsets = [d for d in range(-REACH, REACH + 1) if d != 0]
    peers = [(owner(d), feat) for d in offsets]
    peers += [(blk, lax.rem(feat + s, feats)) for s in range(1, feats)]
    for peer in peers:
        pl.semaphore_signal(barrier, inc=1, device_id=peer, device_id_type=MESH)
    small = [
        pltpu.make_async_copy(source, target, small_sem.at[i]) for i, (source, target) in enumerate(
            ((cols_in, cols), (count_in, count), (weight_in, weight), (bias_in, bias)))]
    for copy in small[:2]:
        copy.start()
    for q in range(STAGES):
        stage_copy(q).start()
    own_copy = pltpu.make_async_copy(ft, raw.at[core, REACH], own_sem)
    own_copy.start()
    for copy in small[2:]:
        copy.start()
    for copy in small[:2]:
        copy.wait()
    pl.semaphore_wait(barrier, len(peers))

    def piece(n):
        return pl.ds(n // CUTS * SUB, SUB), pl.ds(n % CUTS * LANES, LANES)

    def panel_copy(d, n):
        features, nodes = piece(n)
        sign = 1 if d > 0 else -1
        target = REACH + d
        source = target - sign
        src = ft.at[features, nodes] if source == REACH else raw.at[core, source, features, nodes]
        return pltpu.make_async_remote_copy(
            src_ref=src, dst_ref=raw.at[core, target, features, nodes],
            send_sem=panel_send.at[target, n], recv_sem=panel_recv.at[target, n],
            device_id=(owner(-sign), feat), device_id_type=MESH)

    def pair_copy(slot, n):
        features, nodes = piece(n)
        here = raw.at[core, slot, features, nodes]
        return pltpu.make_async_remote_copy(
            src_ref=ft.at[features, nodes] if slot == REACH else here, dst_ref=here,
            send_sem=pair_send.at[slot, n], recv_sem=pair_recv.at[slot, n],
            device_id=partner, device_id_type=MESH)

    def relay(d, n):
        panel_copy(d, n).wait_recv()
        if abs(d) < REACH:
            panel_copy(2 * d, n).start()
        pair_copy(REACH + d, n).start()

    def send_own(n):
        for d in (-1, 1):
            panel_copy(d, n).start()

    for n in range(AHEAD):
        send_own(n)
    for n in range(CHUNKS):
        pair_copy(REACH, n).start()

    for h in range(HALVES):
        scaled[h, SPAN * ROWS] = jnp.zeros((WIDE, TILE), jnp.bfloat16)

    first = (blk - REACH) * ROWS
    blocks = owners * ROWS

    def convert(q):
        slot = q % STAGES
        b = block_row(q)
        used = count[b]
        for t in range(SLOTS):
            local = (cols[t, b] - first + blocks) & (blocks - 1)
            picks[q, t] = jnp.where(t < used, local, SPAN * ROWS)
        stage_copy(q).wait()
        for t in range(SLOTS):
            tiles[q, t * TILE:(t + 1) * TILE] = stage[slot, t].astype(jnp.float32).astype(jnp.bfloat16).T

    def own_row(q, _):
        convert(q)
        n = count[block_row(q)]
        total = jnp.zeros((TILE, TILE), jnp.int32)
        for t in range(SLOTS):
            total = total + stage[q, t] * (t < n).astype(jnp.int32)
        total = total.astype(jnp.float32).astype(jnp.bfloat16)
        ones = jnp.ones((8, TILE), jnp.bfloat16)
        degree = 1.0 + lax.dot_general(ones, total, NT, preferred_element_type=jnp.float32)
        degq[REACH, pl.ds(q, 1)] = degree[0:1]
        stage_copy(q + STAGES).start()
        return 0

    def more_row(q, _):
        convert(q)

        @pl.when(q < HALF - STAGES)
        def _():
            stage_copy(q + STAGES).start()
        return 0

    def degq_copy(d):
        return pltpu.make_async_remote_copy(
            src_ref=degq.at[REACH], dst_ref=degq.at[REACH - d],
            send_sem=degq_send.at[REACH - d], recv_sem=degq_recv.at[REACH - d],
            device_id=(owner(d), feat), device_id_type=MESH)

    def degall_copy(s):
        return pltpu.make_async_remote_copy(
            src_ref=degq, dst_ref=degall.at[feat],
            send_sem=degall_send.at[s], recv_sem=degall_recv.at[s],
            device_id=(blk, lax.rem(feat + s, feats)), device_id_type=MESH)

    def scale(n, *ds):
        h = n // CUTS
        for d in ds:
            pair_copy(REACH + d, n).wait()
        for d in ds:
            slot = REACH + d

            def body(i, _, slot=slot):
                block = n % CUTS * BLOCKS + i
                nodes = pl.ds(pl.multiple_of(block * TILE, TILE), TILE)
                factor = inv[pl.ds(slot * ROWS + block, 1)]
                for k in range(CORES):
                    values = raw[k, slot, h * SUB:(h + 1) * SUB, nodes].astype(jnp.float32)
                    scaled[h, slot * ROWS + block, k * SUB:(k + 1) * SUB] = (values * factor).astype(jnp.bfloat16)
                return 0
            lax.fori_loop(0, BLOCKS, body, 0, unroll=4)

    def agg_copy(h, j, s):
        rows = pl.ds(s * PAIRS, PAIRS)
        return pltpu.make_async_remote_copy(
            src_ref=aggsend.at[h, j, rows], dst_ref=aggrecv.at[rows, h, chip],
            send_sem=agg_send.at[h, j, s], recv_sem=agg_recv.at[h, j, s],
            device_id=(blk, lax.rem(chip + j, CHIPS) * CORES + core), device_id_type=MESH)

    def aggregate_rows(h, s):
        def row(i, _):
            j, k = i // PAIRS, s * PAIRS + i % PAIRS
            q = j * GROUP + k
            b = block_row(q)
            left = jnp.concatenate([scaled[h, picks[q, t]] for t in range(SLOTS)], axis=1)
            total = lax.dot_general(left, tiles[q], NN, preferred_element_type=jnp.float32)
            total = total + scaled[h, REACH * ROWS + b].astype(jnp.float32)
            aggsend[h, j, k] = (total * inv[pl.ds(REACH * ROWS + b, 1)]).astype(jnp.bfloat16)
            return 0
        lax.fori_loop(PAIRS, CHIPS * PAIRS, row, 0, unroll=True)
        for j in (2, 1, 3):
            agg_copy(h, j, s).start()
        lax.fori_loop(0, PAIRS, row, 0, unroll=True)
        rows = pl.ds(s * PAIRS, PAIRS)
        aggrecv[rows, h, chip] = aggsend[h, 0, rows]

    def out_copy(s):
        rows = pl.ds(s * PAIRS * TILE, PAIRS * TILE)
        return pltpu.make_async_copy(out.at[rows], out_hbm.at[rows], out_sem.at[s])

    def finish(s):
        for h in range(HALVES):
            for j in (2, 1, 3):
                agg_copy(h, j, s).wait()
        for k in range(s * PAIRS, (s + 1) * PAIRS):
            values = aggrecv[k].reshape(HALVES * CHIPS * WIDE, TILE).astype(jnp.float32)
            peak_abs = jnp.max(jnp.abs(values))
            normalized = (values / (peak_abs + epsilon)).astype(jnp.bfloat16)
            mixed = lax.dot_general(normalized, order[...], TN, preferred_element_type=jnp.float32)
            out[k * TILE:(k + 1) * TILE] = jnp.maximum(mixed + bias[...], 0.0).astype(jnp.bfloat16)

    def near(n):
        for d in (-1, 1):
            relay(d, n)
        if n + AHEAD < CHUNKS:
            send_own(n + AHEAD)

    def far(n):
        for d in (-2, 2):
            relay(d, n)

    lax.fori_loop(0, GROUP, own_row, 0)
    for d in offsets:
        degq_copy(d).start()
    done = GROUP
    for n in range(CHUNKS):
        near(n)
        if n == DEGREES:
            for d in offsets:
                degq_copy(d).wait()
            for s in range(1, feats):
                degall_copy(s).start()
            degall[feat] = degq[...]
        more = (HALF - GROUP) * (n + 1) // CHUNKS + GROUP
        lax.fori_loop(done, more, more_row, 0)
        done = more
    far(0)
    for s in range(1, feats):
        degall_copy(s).wait()
    for f in range(feats):
        for d in range(SPAN):
            inv[pl.ds(d * ROWS + f * GROUP, GROUP)] = lax.rsqrt(degall[f, d])
    own_copy.wait()
    scale(0, 0, -1, 1)
    far(1)
    scale(1, 0, -1, 1)
    scale(0, -2, 2)
    scale(1, -2, 2)
    aggregate_rows(0, 0)
    scale(2, 0, -1, 1)
    far(2)
    aggregate_rows(0, 1)
    scale(3, 0, -1, 1)
    aggregate_rows(0, 2)
    scale(2, -2, 2)
    for copy in small[2:]:
        copy.wait()
    for x in range(CHIPS):
        for c in range(CORES):
            for h in range(HALVES):
                source = (x * CORES + c) * PART + h * SUB
                target = (h * CHIPS + x) * WIDE + c * SUB
                order[target:target + SUB] = weight[source:source + SUB]
    far(3)
    aggregate_rows(0, 3)
    scale(3, -2, 2)
    for s in range(SUBS):
        aggregate_rows(1, s)
        if s >= 2:
            finish(s - 2)
            out_copy(s - 2).start()
    for s in (SUBS - 2, SUBS - 1):
        finish(s)
        out_copy(s).start()
    for n in range(CHUNKS):
        for d in offsets:
            panel_copy(d, n).wait_send()
    for s in range(SUBS):
        out_copy(s).wait()


def per_device(features, tile_cols, tile_count, edge_mask, weight, bias):
    feats = lax.axis_size("feat")
    hbm = pl.BlockSpec(memory_space=pl.ANY)
    dma = pltpu.SemaphoreType.DMA
    return pl.pallas_call(
        kernel,
        out_shape=jax.ShapeDtypeStruct((GROUP * TILE, weight.shape[1]), jnp.bfloat16),
        in_specs=[hbm] * 6,
        out_specs=hbm,
        scratch_shapes=[
            pltpu.SMEM((SLOTS, ROWS), jnp.int32),
            pltpu.SMEM((ROWS,), jnp.int32),
            pltpu.VMEM(weight.shape, jnp.bfloat16),
            pltpu.VMEM((1, weight.shape[1]), jnp.float32),
            pltpu.VMEM((GROUP * TILE, weight.shape[1]), jnp.bfloat16),
            pltpu.VMEM((STAGES, SLOTS, TILE, TILE), jnp.int32),
            pltpu.VMEM((HALF, SLOTS * TILE, TILE), jnp.bfloat16),
            pltpu.VMEM((CORES, SPAN, PART, NODES), jnp.bfloat16),
            pltpu.VMEM((HALVES, SPAN * ROWS + 1, WIDE, TILE), jnp.bfloat16),
            pltpu.VMEM((SPAN * ROWS, TILE), jnp.float32),
            pltpu.VMEM((SPAN, GROUP, TILE), jnp.float32),
            pltpu.VMEM((feats, SPAN, GROUP, TILE), jnp.float32),
            pltpu.VMEM((HALVES, CHIPS, GROUP, WIDE, TILE), jnp.bfloat16),
            pltpu.VMEM((GROUP, HALVES, CHIPS, WIDE, TILE), jnp.bfloat16),
            pltpu.SMEM((HALF, SLOTS), jnp.int32),
            pltpu.VMEM(weight.shape, jnp.bfloat16),
            dma((4,)), dma((SUBS,)), dma((STAGES,)), dma, dma((SPAN, CHUNKS)), dma((SPAN, CHUNKS)),
            dma((SPAN, CHUNKS)), dma((SPAN, CHUNKS)),
            dma((SPAN,)), dma((SPAN,)), dma((feats,)), dma((feats,)),
            dma((HALVES, CHIPS, SUBS)), dma((HALVES, CHIPS, SUBS)),
        ],
        compiler_params=pltpu.CompilerParams(
            collective_id=0, has_side_effects=True, vmem_limit_bytes=60 * 1024 * 1024),
    )(features.T, edge_mask, tile_cols.T, tile_count, weight, bias.reshape(1, -1))


def solution(mesh):
    placed = (P("blk", "feat"), P("blk", None), P("blk"), P("blk", None, None, None), P(), P())
    return jax.shard_map(
        per_device, mesh=mesh, in_specs=placed, out_specs=P(("blk", "feat"), None), check_vma=False
    )
```
